32 devices in a mesh: dp: 8 (over y, x, core), seq: 4 (over z).
Axes of the slice: x: 2, y: 2, z: 4, core: 2. Of those that a mesh axis runs over, the one named last changes fastest.
Arguments:
- img_qkv: bfloat16 [8, 448, 3, 512], P('dp', 'seq'), may hold values from -6 to 6
- txt_qkv: bfloat16 [8, 64, 3, 512], P('dp', 'seq'), may hold values from -6 to 6
- img_cot: bfloat16 [8, 448, 512], P('dp', 'seq'), may hold values from -48 to 48
- txt_cot: bfloat16 [8, 64, 512], P('dp', 'seq'), may hold values from -48 to 48
- norm_gains: float32 [4, 128], replicated, may hold values from 0.5 to 2
Outputs:
- img_out: bfloat16 [8, 448, 512], P('dp', 'seq')
- txt_out: bfloat16 [8, 64, 512], P('dp', 'seq')
- img_grad: bfloat16 [8, 448, 3, 512], P('dp', 'seq')
- txt_grad: bfloat16 [8, 64, 3, 512], P('dp', 'seq')
- gain_grad: float32 [512], P('dp')
The draws below stay inside these ranges and needn't reach their ends.
All inputs are finite; a program needn't handle non-finite values.
Results may differ from the reference program's by a relative error of at most 0.012.
The reference program's roundings to bfloat16 on the way count: a program that leaves them out, or rounds other values in their place, can miss the bound.
Values may be sent and summed in bfloat16 or wider, within the bound.
No kernel may reach another device: no remote copies, remote signals or barrier semaphores. Data moves between devices by JAX's collectives and lax.ppermute only.
A program may use at most 128 MiB of HBM per device.

```python
import math
import jax
import jax.numpy as jnp
from jax import lax

HD = 128
HEADS = 4
HW = 512
GRID_W = 64
IMG = 448
TXT = 64
SAMPLES = 8


def levels(rng, shape, split, low, top_value):
    gain = 1.0
    for dim, parts in split:
        draws = jax.random.uniform(jax.random.fold_in(jax.random.fold_in(rng, 6), dim), (parts,), jnp.float32, low / len(split), top_value / len(split))
        gain = gain * jnp.repeat(jnp.exp(draws), shape[dim] // parts).reshape((-1,) + (1,) * (len(shape) - 1 - dim))
    return gain


def normal_values(stream_key, shape, width, most, split=(), kind=jnp.bfloat16):
    level = levels(stream_key, shape, split, -0.22, 0.18) if split else 1.0
    drawn = jax.random.normal(stream_key, shape, jnp.float32) * width * level
    return jnp.minimum(jnp.maximum(drawn, -most), most).astype(kind)


def setup_inputs(seed: int = 0) -> dict:
    seeds = jax.random.split(jax.random.key(seed), 6)
    return {
        "img_qkv": normal_values(seeds[0], (SAMPLES, IMG, 3, HW), 1.0, 6.0, ((0, 8), (1, 4))),
        "txt_qkv": normal_values(seeds[1], (SAMPLES, TXT, 3, HW), 1.0, 6.0, ((0, 8), (1, 4))),
        "img_cot": normal_values(seeds[2], (SAMPLES, IMG, HW), 8.0, 48.0, ((0, 8), (1, 4))),
        "txt_cot": normal_values(seeds[3], (SAMPLES, TXT, HW), 8.0, 48.0, ((0, 8), (1, 4))),
        "norm_gains": jnp.clip(jnp.exp(jax.random.uniform(seeds[4], (4, HD), jnp.float32, math.log(0.5), math.log(2.0))), 0.5, 2.0),
    }


EPSILON = 1e-06

def rope_tables(seq_len, text_len, grid_w, head_dim):
    position = jnp.arange(seq_len, dtype=jnp.int32)
    image_pos = jnp.maximum(position - text_len, 0)
    image_col = (position >= text_len).astype(jnp.float32)
    row_pos = (image_pos // grid_w).astype(jnp.float32) * image_col
    col_pos = (image_pos % grid_w).astype(jnp.float32) * image_col
    time_dims = head_dim // 8
    axis_dims = (head_dim - time_dims) // 2
    channel = jnp.arange(head_dim, dtype=jnp.int32)
    in_rows = (channel >= time_dims) & (channel < time_dims + axis_dims)
    in_cols = channel >= time_dims + axis_dims
    within = jnp.where(in_cols, channel - time_dims - axis_dims, channel - time_dims)
    within = jnp.maximum(within, 0) // 2
    frequency = jnp.power(jnp.float32(10000.0), -2.0 * within.astype(jnp.float32) / axis_dims)
    angles = jnp.where(in_rows[None, :], row_pos[:, None] * frequency[None, :], jnp.float32(0.0))
    angles = jnp.where(in_cols[None, :], col_pos[:, None] * frequency[None, :], angles)
    row_idx = channel[:, None]
    col_idx = channel[None, :]
    plus_one = ((row_idx % 2 == 0) & (col_idx == row_idx + 1)).astype(jnp.float32)
    minus_one = ((row_idx % 2 == 1) & (col_idx == row_idx - 1)).astype(jnp.float32)
    swap_mat = plus_one - minus_one
    return (jnp.cos(angles), jnp.sin(angles), swap_mat, image_col[:, None])

def rms_rows(values_in):
    inverse = lax.rsqrt(lax.optimization_barrier(jnp.mean(values_in * values_in, axis=-1, keepdims=True)) + EPSILON)
    return (values_in * inverse, inverse)

def rms_back(grad_hat, hat_vals, inverse):
    middle = lax.optimization_barrier(jnp.mean(grad_hat * hat_vals, axis=-1, keepdims=True))
    return (grad_hat - hat_vals * middle) * inverse

def rotate(values_in, tables):
    cos_t, sin_t, swap_mat, image_col = tables
    turned = jnp.dot(values_in, swap_mat, precision=lax.Precision.HIGHEST)
    return values_in * cos_t + turned * sin_t

def unrotate(grad_in, tables):
    cos_t, sin_t, swap_mat, image_col = tables
    turned = jnp.dot(grad_in * sin_t, swap_mat.T, precision=lax.Precision.HIGHEST)
    return grad_in * cos_t + turned

def head_pass(q_raw, k_raw, value, d_out, norm_gains, tables):
    image_col = tables[3]
    head_dim = q_raw.shape[1]
    attn_scale = 1.0 / math.sqrt(head_dim)
    q_hat, q_inv = rms_rows(q_raw)
    k_hat, k_inv = rms_rows(k_raw)
    q_gain = jnp.where(image_col > 0.5, norm_gains[0][None, :], norm_gains[2][None, :])
    k_gain = jnp.where(image_col > 0.5, norm_gains[1][None, :], norm_gains[3][None, :])
    q_rot = rotate(q_hat * q_gain, tables).astype(jnp.bfloat16)
    k_rot = rotate(k_hat * k_gain, tables).astype(jnp.bfloat16)
    scores = jnp.dot(q_rot, k_rot.T, preferred_element_type=jnp.float32) * attn_scale
    exp_scores = jnp.exp(scores)
    prob_full = exp_scores / lax.optimization_barrier(jnp.sum(exp_scores, axis=1, keepdims=True))
    prob_half = prob_full.astype(jnp.bfloat16)
    attn_out = jnp.dot(prob_half, value, preferred_element_type=jnp.float32).astype(jnp.bfloat16)
    row_delta = lax.optimization_barrier(jnp.sum(d_out.astype(jnp.float32) * attn_out.astype(jnp.float32), axis=1, keepdims=True))
    d_value = jnp.dot(prob_half.T, d_out, preferred_element_type=jnp.float32)
    d_prob = jnp.dot(d_out, value.T, preferred_element_type=jnp.float32)
    d_score = (prob_full * (d_prob - row_delta) * attn_scale).astype(jnp.bfloat16)
    dq_rot = jnp.dot(d_score, k_rot, preferred_element_type=jnp.float32)
    dk_rot = jnp.dot(d_score.T, q_rot, preferred_element_type=jnp.float32)
    dq_norm = unrotate(dq_rot, tables)
    dk_norm = unrotate(dk_rot, tables)
    text_col = 1.0 - image_col
    gain_terms = jnp.stack([lax.optimization_barrier(jnp.sum(dq_norm * q_hat * image_col, axis=0)), lax.optimization_barrier(jnp.sum(dk_norm * k_hat * image_col, axis=0)), lax.optimization_barrier(jnp.sum(dq_norm * q_hat * text_col, axis=0)), lax.optimization_barrier(jnp.sum(dk_norm * k_hat * text_col, axis=0))])
    d_query = rms_back(dq_norm * q_gain, q_hat, q_inv)
    d_key = rms_back(dk_norm * k_gain, k_hat, k_inv)
    return (attn_out, d_query.astype(jnp.bfloat16), d_key.astype(jnp.bfloat16), d_value.astype(jnp.bfloat16), gain_terms)

def reference(img_qkv, txt_qkv, img_cot, txt_cot, norm_gains):
    seq_len = TXT + IMG
    tables = rope_tables(seq_len, TXT, GRID_W, HD)
    joint = jnp.concatenate([txt_qkv, img_qkv], axis=1).reshape(SAMPLES, seq_len, 3, HEADS, HD)
    joint = jnp.transpose(joint, (0, 3, 1, 2, 4)).reshape(SAMPLES * HEADS, seq_len, 3, HD)
    joint_cot = jnp.concatenate([txt_cot, img_cot], axis=1).reshape(SAMPLES, seq_len, HEADS, HD)
    joint_cot = jnp.transpose(joint_cot, (0, 2, 1, 3)).reshape(SAMPLES * HEADS, seq_len, HD)

    def one_head(pieces):
        projected, grad_out = pieces
        return head_pass(projected[:, 0].astype(jnp.float32), projected[:, 1].astype(jnp.float32), projected[:, 2], grad_out, norm_gains, tables)
    attn_out, d_query, d_key, d_value, gain_terms = lax.map(one_head, (joint, joint_cot))
    attn_out = jnp.transpose(attn_out.reshape(SAMPLES, HEADS, seq_len, HD), (0, 2, 1, 3)).reshape(SAMPLES, seq_len, HEADS * HD)
    grads = jnp.stack([d_query, d_key, d_value], axis=2).reshape(SAMPLES, HEADS, seq_len, 3, HD)
    grads = jnp.transpose(grads, (0, 2, 3, 1, 4)).reshape(SAMPLES, seq_len, 3, HEADS * HD)
    grad_scale = 1.0 / math.sqrt(SAMPLES * seq_len * HEADS)
    gain_grad = (lax.optimization_barrier(jnp.sum(gain_terms, axis=0)) * grad_scale).reshape(4 * HD)
    return (attn_out[:, TXT:], attn_out[:, :TXT], grads[:, TXT:], grads[:, :TXT], gain_grad)
```

```python
import functools
import math

import jax
import jax.numpy as jnp
import numpy as np
from jax import lax
from jax.experimental import pallas as pl
from jax.experimental.pallas import tpu as pltpu
from jax.sharding import PartitionSpec as P

HD = 128
GRID_W = 64
EPSILON = 1e-06
LOG2_E = math.log2(math.e)
VMEM_LIMIT = 56 * 1024 * 1024
HBM = pl.BlockSpec(memory_space=pl.ANY)
VMEM = pl.BlockSpec(memory_space=pltpu.VMEM)


def rope_tables(n, txt_rows, img_rows):
    image = np.arange(n * img_rows).reshape(n, img_rows)
    time_dims = HD // 8
    axis_dims = (HD - time_dims) // 2
    channel = np.arange(HD)
    in_rows = (channel >= time_dims) & (channel < time_dims + axis_dims)
    in_cols = channel >= time_dims + axis_dims
    within = np.where(in_cols, channel - time_dims - axis_dims, channel - time_dims)
    within = np.maximum(within, 0) // 2
    frequency = np.power(10000.0, -2.0 * within / axis_dims).astype(np.float32)
    row_pos = (image // GRID_W).astype(np.float32)[..., None]
    col_pos = (image % GRID_W).astype(np.float32)[..., None]
    angles = np.where(in_rows, row_pos * frequency, np.float32(0.0))
    angles = np.where(in_cols, col_pos * frequency, angles)
    angles = np.concatenate([np.zeros((n, txt_rows, HD), np.float32), angles], axis=1)
    angles = angles.reshape(n * (txt_rows + img_rows), HD).astype(np.float64)
    sign = np.where(channel % 2 == 0, -1.0, 1.0)
    return np.cos(angles).astype(np.float32), (np.sin(angles) * sign).astype(np.float32)


def run_copies(copies):
    for copy in copies:
        copy.start()
    for copy in copies:
        copy.wait()


def pack_kernel(n, iq, tq, ic, tc, *refs):
    outs, sems = refs[:n], refs[n]
    txt_rows = tc.shape[1]
    rows = txt_rows + ic.shape[1]
    me = lax.axis_index("seq")
    copies = []
    for step in range(n):
        head = lax.rem(me + step, n)
        cols = pl.ds(pl.multiple_of(head * HD, HD), HD)
        out = outs[step]
        pairs = (
            (tq.at[0, :, :, cols], out.at[0:3, 0:txt_rows]),
            (iq.at[0, :, :, cols], out.at[0:3, txt_rows:rows]),
            (tc.at[0, :, cols], out.at[3, 0:txt_rows]),
            (ic.at[0, :, cols], out.at[3, txt_rows:rows]),
        )
        for i, (src, dst) in enumerate(pairs):
            copies.append(pltpu.make_async_copy(src, dst, sems.at[step, i]))
    run_copies(copies)


def unpack_kernel(n, *refs):
    ins = refs[:n]
    pieces, io, to, ig, tg, gain, sems = refs[n:]
    txt_rows = to.shape[1]
    rows = txt_rows + io.shape[1]
    me = lax.axis_index("seq")
    copies = []
    for step in range(n):
        head = lax.rem(me + step, n)
        cols = pl.ds(pl.multiple_of(head * HD, HD), HD)
        src = ins[step]
        pairs = (
            (src.at[0:3, 0:txt_rows], tg.at[0, :, :, cols]),
            (src.at[0:3, txt_rows:rows], ig.at[0, :, :, cols]),
            (src.at[3, 0:txt_rows], to.at[0, :, cols]),
            (src.at[3, txt_rows:rows], io.at[0, :, cols]),
        )
        for i, (a, b) in enumerate(pairs):
            copies.append(pltpu.make_async_copy(a, b, sems.at[step, i]))
    for copy in copies:
        copy.start()
    gain[...] = jnp.sum(pieces[...], axis=0, keepdims=True)
    for copy in copies:
        copy.wait()


def attend_kernel(n, txt_rows, per, grad_scale, block_rows, *refs):
    ins = refs[:n]
    cos_ref, sin_ref, gains_ref = refs[n : n + 3]
    outs = refs[n + 3 : 2 * n + 3]
    gain_out = refs[2 * n + 3]
    q_rot, k_rot, val, cot, q_hat, k_hat, dq_acc, dk_acc, dv_acc = refs[2 * n + 4 :]
    rows = ins[0].shape[1]
    seq_len = n * rows
    scale = 1.0 / math.sqrt(HD)
    me = lax.axis_index("seq")
    lane = lax.broadcasted_iota(jnp.int32, (rows, HD), 1)
    even = lane % 2 == 0
    is_txt = lax.broadcasted_iota(jnp.int32, (rows, HD), 0) < txt_rows
    gains = gains_ref[...]
    q_gain = jnp.where(is_txt, gains[2:3], gains[0:1])
    k_gain = jnp.where(is_txt, gains[3:4], gains[1:2])
    last = (((1,), (1,)), ((), ()))
    first = (((0,), (0,)), ((), ()))

    def swap(x):
        return jnp.where(even, pltpu.roll(x, HD - 1, 1), pltpu.roll(x, 1, 1))

    def table(step):
        owner = lax.rem(me + (n - step), n)
        at = pl.ds(pl.multiple_of(owner * rows, rows), rows)
        return cos_ref[at, :], sin_ref[at, :]

    inverse = []
    for step in range(n):
        cos, sin = table(step)
        at = slice(step * rows, (step + 1) * rows)
        pair = []
        for slot, gain, hat, rot in ((0, q_gain, q_hat, q_rot), (1, k_gain, k_hat, k_rot)):
            raw = ins[step][slot].astype(jnp.float32)
            inv = lax.rsqrt(jnp.mean(raw * raw, axis=1, keepdims=True) + EPSILON)
            norm = raw * inv
            hat[at] = norm
            norm = norm * gain
            rot[at] = (norm * cos + swap(norm) * sin).astype(jnp.bfloat16)
            pair.append(inv)
        inverse.append(pair)
        val[at] = ins[step][2]
        cot[at] = ins[step][3]

    def block(i, first_block):
        at = pl.ds(pl.multiple_of(i * block_rows, block_rows), block_rows)
        q_b, g_b = q_rot[at, :], cot[at, :]
        k, v = k_rot[...], val[...]
        s = lax.dot_general(q_b, k, last, preferred_element_type=jnp.float32)
        e = jnp.exp2(s * (scale * LOG2_E))
        r = 1.0 / jnp.sum(e, axis=1, keepdims=True)
        p = e * r
        pb = p.astype(jnp.bfloat16)
        o = jnp.dot(pb, v, preferred_element_type=jnp.float32).astype(jnp.bfloat16)
        delta = jnp.sum(g_b.astype(jnp.float32) * o.astype(jnp.float32), axis=1, keepdims=True)
        dp = lax.dot_general(g_b, v, last, preferred_element_type=jnp.float32)
        ds = (p * (dp - delta) * scale).astype(jnp.bfloat16)
        dv = lax.dot_general(pb, g_b, first, preferred_element_type=jnp.float32)
        dq_acc[at, :] = jnp.dot(ds, k, preferred_element_type=jnp.float32)
        dk = lax.dot_general(ds, q_b, first, preferred_element_type=jnp.float32)
        if first_block:
            dv_acc[...] = dv
            dk_acc[...] = dk
        else:
            dv_acc[...] += dv
            dk_acc[...] += dk
        return o

    n_blocks = seq_len // block_rows
    assert block_rows % rows == 0
    per_block = block_rows // rows
    for i in range(n_blocks):
        o = block(i, i == 0)
        for j in range(per_block):
            outs[i * per_block + j][3] = o[j * rows : (j + 1) * rows]

    sums = [jnp.zeros((1, HD), jnp.float32) for _ in range(4)]
    for step in range(n):
        cos, sin = table(step)
        at = slice(step * rows, (step + 1) * rows)
        outs[step][2] = dv_acc[at].astype(jnp.bfloat16)
        for slot, gain, hat_ref, acc in ((0, q_gain, q_hat, dq_acc), (1, k_gain, k_hat, dk_acc)):
            rot_grad = acc[at]
            hat = hat_ref[at]
            inv = inverse[step][slot]
            grad = rot_grad * cos - swap(rot_grad) * sin
            both = grad * hat
            sums[slot] += jnp.sum(both[txt_rows:], axis=0, keepdims=True)
            sums[2 + slot] += jnp.sum(both[:txt_rows], axis=0, keepdims=True)
            middle = jnp.mean(both * gain, axis=1, keepdims=True)
            outs[step][slot] = ((grad * gain - hat * middle) * inv).astype(jnp.bfloat16)

    groups = 4 * HD // per
    for i in range(groups):
        row, off = (i * per) // HD, (i * per) % HD
        piece = sums[row] * grad_scale
        if off:
            piece = pltpu.roll(piece, HD - off, 1)
        gain_out[i * n : (i + 1) * n, :] = jnp.broadcast_to(piece, (n, HD))


def per_device(img_qkv, txt_qkv, img_cot, txt_cot, norm_gains):
    n = lax.axis_size("seq")
    dp = lax.axis_size("dp")
    img_rows, txt_rows = img_cot.shape[1], txt_cot.shape[1]
    width = img_cot.shape[2]
    rows = img_rows + txt_rows
    seq_len = n * rows
    per = 4 * HD // dp
    bf16, f32 = jnp.bfloat16, jnp.float32
    params = pltpu.CompilerParams(vmem_limit_bytes=VMEM_LIMIT)
    block = jax.ShapeDtypeStruct((4, rows, HD), bf16)

    packed = pl.pallas_call(
        functools.partial(pack_kernel, n),
        out_shape=[block] * n,
        in_specs=[HBM] * 4,
        out_specs=[HBM] * n,
        scratch_shapes=[pltpu.SemaphoreType.DMA((n, 4))],
        compiler_params=params,
        name="pack_heads",
    )(jnp.swapaxes(img_qkv, 1, 2), jnp.swapaxes(txt_qkv, 1, 2), img_cot, txt_cot)

    blocks = [packed[0]] + [
        lax.ppermute(packed[d], "seq", [(i, (i + d) % n) for i in range(n)]) for d in range(1, n)
    ]

    cos, sin = rope_tables(n, txt_rows, img_rows)
    grad_scale = 1.0 / math.sqrt(dp * seq_len * (width // HD))
    block_rows = min(seq_len, 512)
    results = pl.pallas_call(
        functools.partial(attend_kernel, n, txt_rows, per, grad_scale, block_rows),
        out_shape=[block] * n + [jax.ShapeDtypeStruct((dp * n, HD), f32)],
        in_specs=[VMEM] * (n + 3),
        out_specs=[VMEM] * (n + 1),
        scratch_shapes=[pltpu.VMEM((seq_len, HD), bf16)] * 4
        + [pltpu.VMEM((seq_len, HD), f32)] * 5,
        compiler_params=params,
        name="attend",
    )(*blocks, jnp.asarray(cos), jnp.asarray(sin), norm_gains)

    back = [results[0]] + [
        lax.ppermute(results[d], "seq", [(i, (i - d) % n) for i in range(n)]) for d in range(1, n)
    ]
    pieces = lax.all_to_all(results[n], ("dp", "seq"), 0, 0, tiled=True)

    io, to, ig, tg, gain = pl.pallas_call(
        functools.partial(unpack_kernel, n),
        out_shape=[
            jax.ShapeDtypeStruct((1, img_rows, width), bf16),
            jax.ShapeDtypeStruct((1, txt_rows, width), bf16),
            jax.ShapeDtypeStruct((1, 3, img_rows, width), bf16),
            jax.ShapeDtypeStruct((1, 3, txt_rows, width), bf16),
            jax.ShapeDtypeStruct((1, HD), f32),
        ],
        in_specs=[HBM] * n + [VMEM],
        out_specs=[HBM] * 4 + [VMEM],
        scratch_shapes=[pltpu.SemaphoreType.DMA((n, 4))],
        compiler_params=params,
        name="unpack_heads",
    )(*back, pieces)
    return io, to, jnp.swapaxes(ig, 1, 2), jnp.swapaxes(tg, 1, 2), gain[0, :per]


def solution(mesh):
    in_specs = (
        P("dp", "seq", None, None),
        P("dp", "seq", None, None),
        P("dp", "seq", None),
        P("dp", "seq", None),
        P(),
    )
    out_specs = (
        P("dp", "seq", None),
        P("dp", "seq", None),
        P("dp", "seq", None, None),
        P("dp", "seq", None, None),
        P("dp"),
    )
    return jax.shard_map(
        per_device, mesh=mesh, in_specs=in_specs, out_specs=out_specs, check_vma=False
    )
```

```python
import functools
import math

import jax
import jax.numpy as jnp
import numpy as np
from jax import lax
from jax.experimental import pallas as pl
from jax.experimental.pallas import tpu as pltpu
from jax.sharding import PartitionSpec as P

HD = 128
GRID_W = 64
EPSILON = 1e-06
LOG2_E = math.log2(math.e)
MIB = 1024 * 1024
VMEM = pl.BlockSpec(memory_space=pltpu.VMEM)


def rope_tables(n, txt_rows, img_rows):
    image = np.arange(n * img_rows).reshape(n, img_rows)
    time_dims = HD // 8
    axis_dims = (HD - time_dims) // 2
    channel = np.arange(HD)
    in_rows = (channel >= time_dims) & (channel < time_dims + axis_dims)
    in_cols = channel >= time_dims + axis_dims
    within = np.where(in_cols, channel - time_dims - axis_dims, channel - time_dims)
    within = np.maximum(within, 0) // 2
    frequency = np.power(10000.0, -2.0 * within / axis_dims).astype(np.float32)
    row_pos = (image // GRID_W).astype(np.float32)[..., None]
    col_pos = (image % GRID_W).astype(np.float32)[..., None]
    angles = np.where(in_rows, row_pos * frequency, np.float32(0.0))
    angles = np.where(in_cols, col_pos * frequency, angles)
    angles = np.concatenate([np.zeros((n, txt_rows, HD), np.float32), angles], axis=1)
    angles = angles.reshape(n * (txt_rows + img_rows), HD).astype(np.float64)
    sign = np.where(channel % 2 == 0, -1.0, 1.0)
    return np.cos(angles).astype(np.float32), (np.sin(angles) * sign).astype(np.float32)


def pack_kernel(n, iq, tq, ic, tc, *refs):
    outs = refs[:n]
    held, sems = refs[n:-1], refs[-1]
    txt_rows = tc.shape[1]
    me = lax.axis_index("seq")
    copies = [
        pltpu.make_async_copy(src, dst, sems.at[i])
        for i, (src, dst) in enumerate(zip((iq, tq, ic, tc), held))
    ]
    for copy in copies:
        copy.start()
    for copy in copies:
        copy.wait()
    iq, tq, ic, tc = held
    for step in range(n):
        head = lax.rem(me + step, n)
        cols = pl.ds(pl.multiple_of(head * HD, HD), HD)
        out = outs[step]
        out[0:3, :txt_rows] = tq[0, :, :, cols]
        out[0:3, txt_rows:] = iq[0, :, :, cols]
        out[3, :txt_rows] = tc[0, :, cols]
        out[3, txt_rows:] = ic[0, :, cols]


def unpack_kernel(n, *refs):
    ins = refs[:n]
    pieces, io, to, ig, tg, gain = refs[n:]
    txt_rows = to.shape[1]
    me = lax.axis_index("seq")
    gain[...] = jnp.sum(pieces[...], axis=0, keepdims=True)[:, : gain.shape[1]]
    for step in range(n):
        head = lax.rem(me + step, n)
        cols = pl.ds(pl.multiple_of(head * HD, HD), HD)
        src = ins[step]
        tg[0, :, :, cols] = src[0:3, :txt_rows]
        ig[0, :, :, cols] = src[0:3, txt_rows:]
        to[0, :, cols] = src[3, :txt_rows]
        io[0, :, cols] = src[3, txt_rows:]


def attend_kernel(n, txt_rows, per, grad_scale, block_rows, *refs):
    ins = refs[:n]
    cos_ref, sin_ref, gains_ref = refs[n : n + 3]
    outs = refs[n + 3 : 2 * n + 3]
    gain_out = refs[2 * n + 3]
    q_rot, k_rot, val, cot, q_hat, k_hat, dq_acc, dk_acc, dv_acc = refs[2 * n + 4 :]
    rows = ins[0].shape[1]
    seq_len = n * rows
    scale = 1.0 / math.sqrt(HD)
    me = lax.axis_index("seq")
    lane = lax.broadcasted_iota(jnp.int32, (rows, HD), 1)
    even = lane % 2 == 0
    is_txt = lax.broadcasted_iota(jnp.int32, (rows, HD), 0) < txt_rows
    gains = gains_ref[...]
    q_gain = jnp.where(is_txt, gains[2:3], gains[0:1])
    k_gain = jnp.where(is_txt, gains[3:4], gains[1:2])
    last = (((1,), (1,)), ((), ()))
    first = (((0,), (0,)), ((), ()))

    def swap(x):
        return jnp.where(even, pltpu.roll(x, HD - 1, 1), pltpu.roll(x, 1, 1))

    def table(step):
        owner = lax.rem(me + (n - step), n)
        at = pl.ds(pl.multiple_of(owner * rows, rows), rows)
        return cos_ref[at, :], sin_ref[at, :]

    inverse = []
    for step in range(n):
        cos, sin = table(step)
        at = slice(step * rows, (step + 1) * rows)
        pair = []
        for slot, gain, hat, rot in ((0, q_gain, q_hat, q_rot), (1, k_gain, k_hat, k_rot)):
            raw = ins[step][slot].astype(jnp.float32)
            inv = lax.rsqrt(jnp.mean(raw * raw, axis=1, keepdims=True) + EPSILON)
            norm = raw * inv
            hat[at] = norm
            norm = norm * gain
            rot[at] = (norm * cos + swap(norm) * sin).astype(jnp.bfloat16)
            pair.append(inv)
        inverse.append(pair)
        val[at] = ins[step][2]
        cot[at] = ins[step][3]

    def block(i, first_block):
        at = pl.ds(pl.multiple_of(i * block_rows, block_rows), block_rows)
        q_b, g_b = q_rot[at, :], cot[at, :]
        k, v = k_rot[...], val[...]
        s = lax.dot_general(q_b, k, last, preferred_element_type=jnp.float32)
        e = jnp.exp2(s * (scale * LOG2_E))
        r = 1.0 / jnp.sum(e, axis=1, keepdims=True)
        p = e * r
        pb = p.astype(jnp.bfloat16)
        o = jnp.dot(pb, v, preferred_element_type=jnp.float32).astype(jnp.bfloat16)
        delta = jnp.sum(g_b.astype(jnp.float32) * o.astype(jnp.float32), axis=1, keepdims=True)
        dp = lax.dot_general(g_b, v, last, preferred_element_type=jnp.float32)
        ds = (p * (dp - delta) * scale).astype(jnp.bfloat16)
        dv = lax.dot_general(pb, g_b, first, preferred_element_type=jnp.float32)
        dq_acc[at, :] = jnp.dot(ds, k, preferred_element_type=jnp.float32)
        dk = lax.dot_general(ds, q_b, first, preferred_element_type=jnp.float32)
        if first_block:
            dv_acc[...] = dv
            dk_acc[...] = dk
        else:
            dv_acc[...] += dv
            dk_acc[...] += dk
        return o

    n_blocks = seq_len // block_rows
    assert block_rows % rows == 0
    per_block = block_rows // rows
    for i in range(n_blocks):
        o = block(i, i == 0)
        for j in range(per_block):
            outs[i * per_block + j][3] = o[j * rows : (j + 1) * rows]

    sums = [jnp.zeros((1, HD), jnp.float32) for _ in range(4)]
    for step in range(n):
        cos, sin = table(step)
        at = slice(step * rows, (step + 1) * rows)
        outs[step][2] = dv_acc[at].astype(jnp.bfloat16)
        for slot, gain, hat_ref, acc in ((0, q_gain, q_hat, dq_acc), (1, k_gain, k_hat, dk_acc)):
            rot_grad = acc[at]
            hat = hat_ref[at]
            inv = inverse[step][slot]
            grad = rot_grad * cos - swap(rot_grad) * sin
            both = grad * hat
            sums[slot] += jnp.sum(both[txt_rows:], axis=0, keepdims=True)
            sums[2 + slot] += jnp.sum(both[:txt_rows], axis=0, keepdims=True)
            middle = jnp.mean(both * gain, axis=1, keepdims=True)
            outs[step][slot] = ((grad * gain - hat * middle) * inv).astype(jnp.bfloat16)

    groups = 4 * HD // per
    for i in range(groups):
        row, off = (i * per) // HD, (i * per) % HD
        piece = sums[row] * grad_scale
        if off:
            piece = pltpu.roll(piece, HD - off, 1)
        gain_out[i * n : (i + 1) * n, :] = jnp.broadcast_to(piece, (n, HD))


def per_device(img_qkv, txt_qkv, img_cot, txt_cot, norm_gains):
    n = lax.axis_size("seq")
    dp = lax.axis_size("dp")
    img_rows, txt_rows = img_cot.shape[1], txt_cot.shape[1]
    width = img_cot.shape[2]
    rows = img_rows + txt_rows
    seq_len = n * rows
    per = 4 * HD // dp
    bf16, f32 = jnp.bfloat16, jnp.float32
    block_rows = min(seq_len, 512)
    params = pltpu.CompilerParams(vmem_limit_bytes=8 * MIB + 32 * block_rows * seq_len)
    block = jax.ShapeDtypeStruct((4, rows, HD), bf16)

    parts = (jnp.swapaxes(img_qkv, 1, 2), jnp.swapaxes(txt_qkv, 1, 2), img_cot, txt_cot)
    packed = pl.pallas_call(
        functools.partial(pack_kernel, n),
        out_shape=[block] * n,
        in_specs=[pl.BlockSpec(memory_space=pltpu.HBM)] * 4,
        out_specs=[VMEM] * n,
        scratch_shapes=[pltpu.VMEM(x.shape, bf16) for x in parts] + [pltpu.SemaphoreType.DMA((4,))],
        compiler_params=params,
        name="pack_heads",
    )(*(pltpu.with_memory_space_constraint(x, pltpu.HBM) for x in parts))

    blocks = [packed[0]] + [
        lax.ppermute(packed[d], "seq", [(i, (i + d) % n) for i in range(n)]) for d in range(1, n)
    ]

    cos, sin = rope_tables(n, txt_rows, img_rows)
    grad_scale = 1.0 / math.sqrt(dp * seq_len * (width // HD))
    results = pl.pallas_call(
        functools.partial(attend_kernel, n, txt_rows, per, grad_scale, block_rows),
        out_shape=[block] * n + [jax.ShapeDtypeStruct((dp * n, HD), f32)],
        in_specs=[VMEM] * (n + 3),
        out_specs=[VMEM] * (n + 1),
        scratch_shapes=[pltpu.VMEM((seq_len, HD), bf16)] * 4
        + [pltpu.VMEM((seq_len, HD), f32)] * 5,
        compiler_params=params,
        name="attend",
    )(*blocks, jnp.asarray(cos), jnp.asarray(sin), norm_gains)

    back = [results[0]] + [
        lax.ppermute(results[d], "seq", [(i, (i - d) % n) for i in range(n)]) for d in range(1, n)
    ]
    pieces = lax.all_to_all(results[n], ("dp", "seq"), 0, 0, tiled=True)

    io, to, ig, tg, gain = pl.pallas_call(
        functools.partial(unpack_kernel, n),
        out_shape=[
            jax.ShapeDtypeStruct((1, img_rows, width), bf16),
            jax.ShapeDtypeStruct((1, txt_rows, width), bf16),
            jax.ShapeDtypeStruct((1, 3, img_rows, width), bf16),
            jax.ShapeDtypeStruct((1, 3, txt_rows, width), bf16),
            jax.ShapeDtypeStruct((1, per), f32),
        ],
        in_specs=[VMEM] * (n + 1),
        out_specs=[VMEM] * 5,
        compiler_params=params,
        name="unpack_heads",
    )(*back, pieces)
    return io, to, jnp.swapaxes(ig, 1, 2), jnp.swapaxes(tg, 1, 2), gain.reshape(per)


def solution(mesh):
    in_specs = (
        P("dp", "seq", None, None),
        P("dp", "seq", None, None),
        P("dp", "seq", None),
        P("dp", "seq", None),
        P(),
    )
    out_specs = (
        P("dp", "seq", None),
        P("dp", "seq", None),
        P("dp", "seq", None, None),
        P("dp", "seq", None, None),
        P("dp"),
    )
    return jax.shard_map(
        per_device, mesh=mesh, in_specs=in_specs, out_specs=out_specs, check_vma=False
    )
```

```python
import functools
import math

import jax
import jax.numpy as jnp
import numpy as np
from jax import lax
from jax.experimental import pallas as pl
from jax.experimental.pallas import tpu as pltpu
from jax.sharding import PartitionSpec as P

HD = 128
GRID_W = 64
EPSILON = 1e-06
LOG2_E = math.log2(math.e)
SCALE = 1.0 / math.sqrt(HD)
MIB = 1024 * 1024
VMEM = pl.BlockSpec(memory_space=pltpu.VMEM)
LAST = (((1,), (1,)), ((), ()))
FIRST = (((0,), (0,)), ((), ()))
bf16, f32 = jnp.bfloat16, jnp.float32


def rope_tables(n, txt_rows, img_rows):
    image = np.arange(n * img_rows).reshape(n, img_rows)
    time_dims = HD // 8
    axis_dims = (HD - time_dims) // 2
    channel = np.arange(HD)
    in_rows = (channel >= time_dims) & (channel < time_dims + axis_dims)
    in_cols = channel >= time_dims + axis_dims
    within = np.where(in_cols, channel - time_dims - axis_dims, channel - time_dims)
    within = np.maximum(within, 0) // 2
    frequency = np.power(10000.0, -2.0 * within / axis_dims).astype(np.float32)
    row_pos = (image // GRID_W).astype(np.float32)[..., None]
    col_pos = (image % GRID_W).astype(np.float32)[..., None]
    angles = np.where(in_rows, row_pos * frequency, np.float32(0.0))
    angles = np.where(in_cols, col_pos * frequency, angles)
    angles = np.concatenate([np.zeros((n, txt_rows, HD), np.float32), angles], axis=1)
    angles = angles.reshape(n * (txt_rows + img_rows), HD).astype(np.float64)
    sign = np.where(channel % 2 == 0, -1.0, 1.0)
    return np.cos(angles).astype(np.float32), (np.sin(angles) * sign).astype(np.float32)


def pair_swap():
    row = lax.broadcasted_iota(jnp.int32, (HD, HD), 0)
    col = lax.broadcasted_iota(jnp.int32, (HD, HD), 1)
    other = jnp.where(col % 2 == 0, col + 1, col - 1)
    return (row == other).astype(f32).astype(bf16)


def lane_sum(x):
    high = x.astype(bf16)
    low = (x - high.astype(f32)).astype(bf16)
    return jnp.dot(
        jnp.concatenate([high, low], axis=1),
        jnp.ones((2 * HD, HD), bf16),
        preferred_element_type=f32,
    )


def wide(x, width):
    return jnp.concatenate([x] * (width // HD), axis=1)


def pack_kernel(n, iq, tq, ic, tc, *refs):
    outs, cots = refs[:n], refs[n : 2 * n - 2]
    held, sems = refs[2 * n - 2 : -1], refs[-1]
    txt_rows = tc.shape[1]
    me = lax.axis_index("seq")
    copies = [
        pltpu.make_async_copy(src, dst, sems.at[i])
        for i, (src, dst) in enumerate(zip((iq, tq, ic, tc), held))
    ]
    for copy in copies:
        copy.start()
    for copy in copies:
        copy.wait()
    iq, tq, ic, tc = held
    for step in range(n):
        head = lax.rem(me + step, n)
        cols = pl.ds(pl.multiple_of(head * HD, HD), HD)
        outs[step][:3, :txt_rows] = tq[0, :, :, cols]
        outs[step][:3, txt_rows:] = iq[0, :, :, cols]
        cot = outs[step].at[3] if step < 2 else cots[step - 2]
        cot[:txt_rows] = tc[0, :, cols]
        cot[txt_rows:] = ic[0, :, cols]


def unpack_kernel(n, *refs):
    ins = refs[:n]
    pieces, io, to, ig, tg, gain = refs[n:]
    txt_rows = to.shape[1]
    me = lax.axis_index("seq")
    gain[...] = jnp.sum(pieces[...], axis=0, keepdims=True)[:, : gain.shape[1]]
    for step in range(n):
        head = lax.rem(me + step, n)
        cols = pl.ds(pl.multiple_of(head * HD, HD), HD)
        src = ins[step]
        tg[0, :, :, cols] = src[0:3, :txt_rows]
        ig[0, :, :, cols] = src[0:3, txt_rows:]
        to[0, :, cols] = src[3, :txt_rows]
        io[0, :, cols] = src[3, txt_rows:]


def table_kernel(n, txt_rows, cos_ref, sin_ref, gains_ref, cos_out, sin_out, *gain_tables):
    rows = cos_ref.shape[0] // n
    me = lax.axis_index("seq")
    gains = gains_ref[...]
    lane = lax.broadcasted_iota(jnp.int32, gains.shape, 1)
    swapped = jnp.where(lane % 2 == 0, pltpu.roll(gains, HD - 1, 1), pltpu.roll(gains, 1, 1))
    is_txt = lax.broadcasted_iota(jnp.int32, (rows, HD), 0) < txt_rows
    for step in range(n):
        owner = lax.rem(me + (n - step), n)
        src = pl.ds(pl.multiple_of(owner * rows, rows), rows)
        dst = slice(step * rows, (step + 1) * rows)
        cos, sin = cos_ref[src, :], sin_ref[src, :]
        cos_out[dst] = cos
        sin_out[dst] = sin
        for slot in range(2):
            gain_tables[2 * slot][dst] = cos * jnp.where(
                is_txt, gains[2 + slot : 3 + slot], gains[slot : slot + 1]
            )
            gain_tables[2 * slot + 1][dst] = sin * jnp.where(
                is_txt, swapped[2 + slot : 3 + slot], swapped[slot : slot + 1]
            )


def forward_kernel(n, block_rows, *refs):
    ins, tables = refs[:n], refs[n : n + 4]
    outs = refs[n + 4 : 2 * n + 4]
    q_rot, k_rot, q_inv, k_inv, prob = refs[2 * n + 4 :]
    rows = ins[0].shape[1]
    seq_len = n * rows
    swap = pair_swap()
    for slot, rot_ref, inv_ref in ((0, q_rot, q_inv), (1, k_rot, k_inv)):
        raw = jnp.concatenate([ins[step][slot] for step in range(n)], axis=0)
        wide_raw = raw.astype(f32)
        inv = lax.rsqrt(lane_sum(wide_raw * wide_raw) * (1.0 / HD) + EPSILON)
        other = jnp.dot(raw, swap, preferred_element_type=f32)
        rot = wide_raw * tables[2 * slot][...] + other * tables[2 * slot + 1][...]
        rot = (rot * inv).astype(bf16)
        inv_ref[...] = inv
        rot_ref[:, :HD] = rot
        rot_ref[:, HD:] = jnp.dot(rot, swap, preferred_element_type=f32).astype(bf16)
    k = k_rot[:, :HD]
    v = jnp.concatenate([ins[step][2] for step in range(n)], axis=0)
    per_block = block_rows // rows
    for i in range(seq_len // block_rows):
        at = slice(i * block_rows, (i + 1) * block_rows)
        s = lax.dot_general(q_rot[at, :HD], k, LAST, preferred_element_type=f32)
        e = jnp.exp2(s * (SCALE * LOG2_E))
        total = sum(e[:, j * HD : (j + 1) * HD] for j in range(seq_len // HD))
        p = e * wide(1.0 / lane_sum(total), seq_len)
        prob[at, :] = p
        o = jnp.dot(p.astype(bf16), v, preferred_element_type=f32).astype(bf16)
        for j in range(per_block):
            outs[i * per_block + j][...] = o[j * rows : (j + 1) * rows]


def backward_kernel(n, txt_rows, per, grad_scale, block_rows, *refs):
    ins, cots, refs = refs[:n], refs[n : 2 * n - 2], refs[2 * n - 2 :]
    cots = [ins[j].at[3] for j in range(2)] + list(cots)
    outs, refs = refs[:n], refs[n:]
    q_rot, k_rot, q_inv, k_inv, prob, cos_ref, sin_ref, gains_ref = refs[:8]
    grads, gain_out = refs[8 : n + 8], refs[n + 8]
    q_acc, k_acc, v_acc = refs[n + 9 :]
    rows = ins[0].shape[1]
    seq_len = n * rows
    v = jnp.concatenate([ins[step][2] for step in range(n)], axis=0)
    per_block = block_rows // rows
    for i in range(seq_len // block_rows):
        at = slice(i * block_rows, (i + 1) * block_rows)
        mine = range(i * per_block, (i + 1) * per_block)
        g = jnp.concatenate([cots[j][...] for j in mine], axis=0)
        o = jnp.concatenate([outs[j][...] for j in mine], axis=0)
        delta = lane_sum(g.astype(f32) * o.astype(f32))
        p = prob[at, :]
        dp = lax.dot_general(g, v, LAST, preferred_element_type=f32)
        ds = (p * (dp - wide(delta, seq_len)) * SCALE).astype(bf16)
        dv = lax.dot_general(p.astype(bf16), g, FIRST, preferred_element_type=f32)
        q_acc[at, :] = jnp.dot(ds, k_rot[...], preferred_element_type=f32)
        dk = lax.dot_general(ds, q_rot[at, :], FIRST, preferred_element_type=f32)
        if i == 0:
            v_acc[...] = dv
            k_acc[...] = dk
        else:
            v_acc[...] += dv
            k_acc[...] += dk

    gains = gains_ref[...]
    is_txt = lax.broadcasted_iota(jnp.int32, (rows, HD), 0) < txt_rows
    sums = [jnp.zeros((1, HD), f32) for _ in range(4)]
    for slot, acc, inv_ref in ((0, q_acc, q_inv), (1, k_acc, k_inv)):
        gain = jnp.where(is_txt, gains[2 + slot : 3 + slot], gains[slot : slot + 1])
        for step in range(n):
            at = slice(step * rows, (step + 1) * rows)
            inv = inv_ref[at, :]
            hat = ins[step][slot].astype(f32) * inv
            grad = acc[at, :HD] * cos_ref[at, :] - acc[at, HD:] * sin_ref[at, :]
            both = grad * hat
            sums[slot] += jnp.sum(both[txt_rows:], axis=0, keepdims=True)
            sums[2 + slot] += jnp.sum(both[:txt_rows], axis=0, keepdims=True)
            middle = lane_sum(both * gain) * (1.0 / HD)
            grads[step][slot] = ((grad * gain - hat * middle) * inv).astype(bf16)
    for step in range(n):
        grads[step][2] = v_acc[step * rows : (step + 1) * rows].astype(bf16)
        grads[step][3] = outs[step][...]

    for i in range(4 * HD // per):
        row, off = (i * per) // HD, (i * per) % HD
        piece = sums[row] * grad_scale
        if off:
            piece = pltpu.roll(piece, HD - off, 1)
        gain_out[i * n : (i + 1) * n, :] = jnp.broadcast_to(piece, (n, HD))


def per_device(img_qkv, txt_qkv, img_cot, txt_cot, norm_gains):
    n = lax.axis_size("seq")
    dp = lax.axis_size("dp")
    img_rows, txt_rows = img_cot.shape[1], txt_cot.shape[1]
    width = img_cot.shape[2]
    rows = img_rows + txt_rows
    seq_len = n * rows
    per = 4 * HD // dp
    block_rows = min(seq_len, 512)
    limit = 8 * MIB + 32 * block_rows * seq_len + 4 * seq_len * seq_len

    def call(kernel, name, operands, out_shape, scratch=(), in_specs=None):
        return pl.pallas_call(
            kernel,
            out_shape=out_shape,
            in_specs=in_specs or [VMEM] * len(operands),
            out_specs=[VMEM] * len(out_shape),
            scratch_shapes=list(scratch),
            compiler_params=pltpu.CompilerParams(vmem_limit_bytes=limit),
            name=name,
        )(*operands)

    def send(block, d, sign):
        return lax.ppermute(block, "seq", [(i, (i + sign * d) % n) for i in range(n)])

    def exchange(blocks, sign):
        return [blocks[0]] + [send(blocks[d], d, sign) for d in range(1, n)]

    def shape(dims, dtype=f32):
        return jax.ShapeDtypeStruct(dims, dtype)

    block = shape((4, rows, HD), bf16)
    three, one = shape((3, rows, HD), bf16), shape((rows, HD), bf16)
    parts = (jnp.swapaxes(img_qkv, 1, 2), jnp.swapaxes(txt_qkv, 1, 2), img_cot, txt_cot)
    packed = call(
        functools.partial(pack_kernel, n),
        "pack_heads",
        [pltpu.with_memory_space_constraint(x, pltpu.HBM) for x in parts],
        [block] * 2 + [three] * (n - 2) + [one] * (n - 2),
        [pltpu.VMEM(x.shape, bf16) for x in parts] + [pltpu.SemaphoreType.DMA((4,))],
        [pl.BlockSpec(memory_space=pltpu.HBM)] * 4,
    )
    cos, sin = rope_tables(n, txt_rows, img_rows)
    qkv = exchange(packed[:n], 1)
    cot = [send(packed[n + i], 2 + i, 1) for i in range(n - 2)]
    tables = call(
        functools.partial(table_kernel, n, txt_rows),
        "rope_tables",
        (jnp.asarray(cos), jnp.asarray(sin), norm_gains),
        [shape((seq_len, HD))] * 6,
    )
    forward = call(
        functools.partial(forward_kernel, n, block_rows),
        "forward",
        (*qkv, *tables[2:]),
        [one] * n
        + [shape((seq_len, 2 * HD), bf16)] * 2
        + [shape((seq_len, HD))] * 2
        + [shape((seq_len, seq_len))],
    )
    grad_scale = 1.0 / math.sqrt(dp * seq_len * (width // HD))
    backward = call(
        functools.partial(backward_kernel, n, txt_rows, per, grad_scale, block_rows),
        "backward",
        (*qkv, *cot, *forward, *tables[:2], norm_gains),
        [block] * n + [shape((dp * n, HD))],
        [pltpu.VMEM((seq_len, 2 * HD), f32)] * 2 + [pltpu.VMEM((seq_len, HD), f32)],
    )
    grads = exchange(backward[:n], -1)
    pieces = lax.all_to_all(backward[n], ("dp", "seq"), 0, 0, tiled=True)
    io, to, ig, tg, gain = call(
        functools.partial(unpack_kernel, n),
        "unpack_heads",
        (*grads, pieces),
        [
            shape((1, img_rows, width), bf16),
            shape((1, txt_rows, width), bf16),
            shape((1, 3, img_rows, width), bf16),
            shape((1, 3, txt_rows, width), bf16),
            shape((1, per)),
        ],
    )
    return io, to, jnp.swapaxes(ig, 1, 2), jnp.swapaxes(tg, 1, 2), gain.reshape(per)


def solution(mesh):
    in_specs = (
        P("dp", "seq", None, None),
        P("dp", "seq", None, None),
        P("dp", "seq", None),
        P("dp", "seq", None),
        P(),
    )
    out_specs = (
        P("dp", "seq", None),
        P("dp", "seq", None),
        P("dp", "seq", None, None),
        P("dp", "seq", None, None),
        P("dp"),
    )
    return jax.shard_map(
        per_device, mesh=mesh, in_specs=in_specs, out_specs=out_specs, check_vma=False
    )
```

```python
import functools
import math

import jax
import jax.numpy as jnp
import numpy as np
from jax import lax
from jax.experimental import pallas as pl
from jax.experimental.pallas import tpu as pltpu
from jax.sharding import PartitionSpec as P

HD = 128
GRID_W = 64
GAIN_ROWS = 16
EPSILON = 1e-06
LOG2_E = math.log2(math.e)
SCALE = 1.0 / math.sqrt(HD)
MIB = 1024 * 1024
VMEM = pl.BlockSpec(memory_space=pltpu.VMEM)
LAST = (((1,), (1,)), ((), ()))
FIRST = (((0,), (0,)), ((), ()))
bf16, f32 = jnp.bfloat16, jnp.float32


def distances(n):
    return sorted(range(n), key=lambda d: (min(d, n - d), d))


def rope_tables(n, txt_rows, img_rows):
    image = np.arange(n * img_rows).reshape(n, img_rows)
    time_dims = HD // 8
    axis_dims = (HD - time_dims) // 2
    channel = np.arange(HD)
    in_rows = (channel >= time_dims) & (channel < time_dims + axis_dims)
    in_cols = channel >= time_dims + axis_dims
    within = np.where(in_cols, channel - time_dims - axis_dims, channel - time_dims)
    within = np.maximum(within, 0) // 2
    frequency = np.power(10000.0, -2.0 * within / axis_dims).astype(np.float32)
    row_pos = (image // GRID_W).astype(np.float32)[..., None]
    col_pos = (image % GRID_W).astype(np.float32)[..., None]
    angles = np.where(in_rows, row_pos * frequency, np.float32(0.0))
    angles = np.where(in_cols, col_pos * frequency, angles)
    angles = np.concatenate([np.zeros((n, txt_rows, HD), np.float32), angles], axis=1)
    angles = angles.reshape(n * (txt_rows + img_rows), HD).astype(np.float64)
    sign = np.where(channel % 2 == 0, -1.0, 1.0)
    return np.cos(angles).astype(np.float32), (np.sin(angles) * sign).astype(np.float32)


def pair_swap():
    row = lax.broadcasted_iota(jnp.int32, (2 * HD, 2 * HD), 0)
    col = lax.broadcasted_iota(jnp.int32, (2 * HD, 2 * HD), 1)
    other = jnp.where(col % 2 == 0, col + 1, col - 1)
    return (row == other).astype(f32).astype(bf16)


def lane_sum(x):
    return jnp.sum(x, axis=1, keepdims=True)


def pack_kernel(n, iq, tq, ic, tc, *refs):
    outs, cots = refs[:n], refs[n : 2 * n - 1]
    held, sems = refs[2 * n - 1 : -1], refs[-1]
    txt_rows = tc.shape[1]
    me = lax.axis_index("seq")
    copies = [
        pltpu.make_async_copy(src, dst, sems.at[i])
        for i, (src, dst) in enumerate(zip((iq, tq, ic, tc), held))
    ]
    for copy in copies:
        copy.start()
    for copy in copies:
        copy.wait()
    iq, tq, ic, tc = held
    for step in range(n):
        head = lax.rem(me + distances(n)[step], n)
        cols = pl.ds(pl.multiple_of(head * HD, HD), HD)
        outs[step][:3, :txt_rows] = tq[0, :, :, cols]
        outs[step][:3, txt_rows:] = iq[0, :, :, cols]
        cot = outs[step].at[3] if step < 1 else cots[step - 1]
        cot[:txt_rows] = tc[0, :, cols]
        cot[txt_rows:] = ic[0, :, cols]


def unpack_kernel(n, *refs):
    ins, parts = refs[:n], refs[n:-5]
    io, to, ig, tg, gain = refs[-5:]
    txt_rows = to.shape[1]
    rows = txt_rows + io.shape[1]
    total = sum(part[...] for part in parts)
    owner = lax.broadcasted_iota(jnp.int32, total.shape, 0) == lax.axis_index("dp")
    total = jnp.sum(jnp.where(owner, total, 0.0), axis=0, keepdims=True)
    gain[...] = total[:, : gain.shape[1]]
    me = lax.axis_index("seq")
    for step in range(n):
        head = lax.rem(me + distances(n)[step], n)
        cols = pl.ds(pl.multiple_of(head * HD, HD), HD)
        for slot in range(4):
            txt, img = (to, io) if slot == 3 else (tg.at[:, slot], ig.at[:, slot])
            at = slot * rows
            txt[0, :, cols] = ins[step][at : at + txt_rows]
            img[0, :, cols] = ins[step][at + txt_rows : at + rows]


def table_kernel(n, txt_rows, cos_ref, sin_ref, gains_ref, cos_out, sin_out, *gain_tables):
    rows = cos_ref.shape[0] // n
    me = lax.axis_index("seq")
    gains = gains_ref[...]
    lane = lax.broadcasted_iota(jnp.int32, gains.shape, 1)
    swapped = jnp.where(lane % 2 == 0, pltpu.roll(gains, HD - 1, 1), pltpu.roll(gains, 1, 1))
    is_txt = lax.broadcasted_iota(jnp.int32, (rows, HD), 0) < txt_rows
    for step in range(n):
        owner = lax.rem(me + (n - distances(n)[step]), n)
        src = pl.ds(pl.multiple_of(owner * rows, rows), rows)
        dst = slice(step * rows, (step + 1) * rows)
        cos, sin = cos_ref[src, :], sin_ref[src, :]
        cos_out[dst] = cos
        sin_out[dst] = sin
        for slot in range(2):
            gain_tables[2 * slot][dst] = cos * jnp.where(
                is_txt, gains[2 + slot : 3 + slot], gains[slot : slot + 1]
            )
            gain_tables[2 * slot + 1][dst] = sin * jnp.where(
                is_txt, swapped[2 + slot : 3 + slot], swapped[slot : slot + 1]
            )


def forward_kernel(n, block_rows, *refs):
    ins, tables = refs[:n], refs[n : n + 4]
    outs = refs[n + 4 : 2 * n + 4]
    q_rot, k_rot, q_inv, k_inv, prob = refs[2 * n + 4 :]
    rows = ins[0].shape[1]
    seq_len = n * rows
    swap = pair_swap()
    raws = [jnp.concatenate([ins[step][slot] for step in range(n)], axis=0) for slot in range(2)]
    others = jnp.dot(jnp.concatenate(raws, axis=1), swap, preferred_element_type=f32)
    rots = []
    for slot, rot_ref, inv_ref in ((0, q_rot, q_inv), (1, k_rot, k_inv)):
        raw = raws[slot].astype(f32)
        inv = lax.rsqrt(lane_sum(raw * raw) * (1.0 / HD) + EPSILON)
        other = others[:, slot * HD : (slot + 1) * HD]
        rot = raw * tables[2 * slot][...] + other * tables[2 * slot + 1][...]
        rot = (rot * inv).astype(bf16)
        inv_ref[...] = jnp.broadcast_to(inv, inv_ref.shape)
        rot_ref[:, :HD] = rot
        rots.append(rot)
    turned = jnp.dot(jnp.concatenate(rots, axis=1), swap, preferred_element_type=f32).astype(bf16)
    q_rot[:, HD:] = turned[:, :HD]
    k_rot[:, HD:] = turned[:, HD:]
    k = k_rot[:, :HD]
    v = jnp.concatenate([ins[step][2] for step in range(n)], axis=0)
    per_block = block_rows // rows
    for i in range(seq_len // block_rows):
        at = slice(i * block_rows, (i + 1) * block_rows)
        s = lax.dot_general(q_rot[at, :HD], k, LAST, preferred_element_type=f32)
        e = jnp.exp2(s * (SCALE * LOG2_E))
        total = sum(e[:, j * HD : (j + 1) * HD] for j in range(seq_len // HD))
        p = e * (1.0 / lane_sum(total))
        prob[at, :] = p
        o = jnp.dot(p.astype(bf16), v, preferred_element_type=f32).astype(bf16)
        for j in range(per_block):
            outs[i * per_block + j][...] = o[j * rows : (j + 1) * rows]


def backward_kernel(n, txt_rows, grad_scale, block_rows, *refs):
    rows = refs[0].shape[1]
    ins, cots, refs = refs[:n], refs[n : 2 * n - 1], refs[2 * n - 1 :]
    cots = [ins[j].at[3] for j in range(1)] + list(cots)
    outs, refs = refs[:n], refs[n:]
    q_rot, k_rot, q_inv, k_inv, prob, cos_ref, sin_ref, gains_ref = refs[:8]
    blocks, gain_out = refs[8 : n + 8], refs[n + 8]
    grads = [
        [block.at[slot * rows : (slot + 1) * rows] for slot in range(4)] for block in blocks
    ]
    q_acc, k_acc, v_acc = refs[n + 9 :]
    seq_len = n * rows
    v = jnp.concatenate([ins[step][2] for step in range(n)], axis=0)
    per_block = block_rows // rows
    for i in range(seq_len // block_rows):
        at = slice(i * block_rows, (i + 1) * block_rows)
        mine = range(i * per_block, (i + 1) * per_block)
        g = jnp.concatenate([cots[j][...] for j in mine], axis=0)
        o = jnp.concatenate([outs[j][...] for j in mine], axis=0)
        delta = lane_sum(g.astype(f32) * o.astype(f32))
        p = prob[at, :]
        dp = lax.dot_general(g, v, LAST, preferred_element_type=f32)
        ds = (p * (dp - delta) * SCALE).astype(bf16)
        dv = lax.dot_general(p.astype(bf16), g, FIRST, preferred_element_type=f32)
        q_acc[at, :] = jnp.dot(ds, k_rot[...], preferred_element_type=f32)
        dk = lax.dot_general(ds, q_rot[at, :], FIRST, preferred_element_type=f32)
        if i == 0:
            v_acc[...] = dv
            k_acc[...] = dk
        else:
            v_acc[...] += dv
            k_acc[...] += dk

    gains = gains_ref[...]
    is_txt = lax.broadcasted_iota(jnp.int32, (rows, HD), 0) < txt_rows
    sums = [jnp.zeros((1, HD), f32) for _ in range(4)]
    for slot, acc, inv_ref in ((0, q_acc, q_inv), (1, k_acc, k_inv)):
        gain = jnp.where(is_txt, gains[2 + slot : 3 + slot], gains[slot : slot + 1])
        for step in range(n):
            at = slice(step * rows, (step + 1) * rows)
            inv = inv_ref[at, :]
            hat = ins[step][slot].astype(f32) * inv
            grad = acc[at, :HD] * cos_ref[at, :] - acc[at, HD:] * sin_ref[at, :]
            both = grad * hat
            sums[slot] += jnp.sum(both[txt_rows:], axis=0, keepdims=True)
            sums[2 + slot] += jnp.sum(both[:txt_rows], axis=0, keepdims=True)
            middle = lane_sum(both * gain) * (1.0 / HD)
            grads[step][slot][...] = ((grad * gain - hat * middle) * inv).astype(bf16)
    for step in range(n):
        grads[step][2][...] = v_acc[step * rows : (step + 1) * rows].astype(bf16)
        grads[step][3][...] = outs[step][...]

    total = jnp.concatenate(sums, axis=0) * grad_scale
    high = total.astype(bf16).astype(f32)
    terms = jnp.concatenate([high, total - high, jnp.zeros((GAIN_ROWS - 8, HD), f32)], axis=0)
    blocks[1][4 * rows :] = terms.astype(bf16)
    gain_out[...] = total


def share_kernel(n, per, first, *refs):
    tail = first[first.shape[0] - GAIN_ROWS :].astype(f32)
    total = tail[:4] + tail[4:8]
    for part in refs[:-1]:
        total += part[...]
    out = refs[-1]
    for i in range(4 * HD // per):
        row, off = (i * per) // HD, (i * per) % HD
        piece = total[row : row + 1]
        out[i : i + 1, :] = pltpu.roll(piece, HD - off, 1) if off else piece


def per_device(img_qkv, txt_qkv, img_cot, txt_cot, norm_gains):
    n = lax.axis_size("seq")
    dp = lax.axis_size("dp")
    img_rows, txt_rows = img_cot.shape[1], txt_cot.shape[1]
    width = img_cot.shape[2]
    rows = img_rows + txt_rows
    seq_len = n * rows
    per = 4 * HD // dp
    block_rows = min(seq_len, 512)
    limit = 8 * MIB + 32 * block_rows * seq_len + 4 * seq_len * seq_len

    def call(kernel, name, operands, out_shape, scratch=(), in_specs=None, flops=None):
        cost = flops and pl.CostEstimate(flops=flops, bytes_accessed=MIB, transcendentals=0)
        return pl.pallas_call(
            kernel,
            out_shape=out_shape,
            in_specs=in_specs or [VMEM] * len(operands),
            out_specs=[VMEM] * len(out_shape),
            scratch_shapes=list(scratch),
            compiler_params=pltpu.CompilerParams(vmem_limit_bytes=limit),
            cost_estimate=cost,
            name=name,
        )(*operands)

    def send(block, d, sign):
        hop = sign * distances(n)[d]
        return lax.ppermute(block, "seq", [(i, (i + hop) % n) for i in range(n)])

    def exchange(blocks, sign):
        return [blocks[0]] + [send(blocks[d], d, sign) for d in range(1, n)]

    def shape(dims, dtype=f32):
        return jax.ShapeDtypeStruct(dims, dtype)

    block = shape((4, rows, HD), bf16)
    three, one = shape((3, rows, HD), bf16), shape((rows, HD), bf16)
    parts = (jnp.swapaxes(img_qkv, 1, 2), jnp.swapaxes(txt_qkv, 1, 2), img_cot, txt_cot)
    packed = call(
        functools.partial(pack_kernel, n),
        "pack_heads",
        [pltpu.with_memory_space_constraint(x, pltpu.HBM) for x in parts],
        [block] * 1 + [three] * (n - 1) + [one] * (n - 1),
        [pltpu.VMEM(x.shape, bf16) for x in parts] + [pltpu.SemaphoreType.DMA((4,))],
        [pl.BlockSpec(memory_space=pltpu.HBM)] * 4,
    )
    cos, sin = rope_tables(n, txt_rows, img_rows)
    qkv = exchange(packed[:n], 1)
    cot = [send(packed[n + i], 1 + i, 1) for i in range(n - 1)]
    tables = call(
        functools.partial(table_kernel, n, txt_rows),
        "rope_tables",
        (jnp.asarray(cos), jnp.asarray(sin), norm_gains),
        [shape((seq_len, HD))] * 6,
    )
    forward = call(
        functools.partial(forward_kernel, n, block_rows),
        "forward",
        (*qkv, *tables[2:]),
        [one] * n
        + [shape((seq_len, 2 * HD), bf16)] * 2
        + [shape((seq_len, HD))] * 2
        + [shape((seq_len, seq_len))],
    )
    grad_scale = 1.0 / math.sqrt(dp * seq_len * (width // HD))
    backward = call(
        functools.partial(backward_kernel, n, txt_rows, grad_scale, block_rows),
        "backward",
        (*qkv, *cot, *forward, *tables[:2], norm_gains),
        [shape((4 * rows + (GAIN_ROWS if step == 1 else 0), HD), bf16) for step in range(n)]
        + [shape((4, HD))],
        [pltpu.VMEM((seq_len, 2 * HD), f32)] * 2 + [pltpu.VMEM((seq_len, HD), f32)],
    )
    first = send(backward[1], 1, -1)
    small = [backward[n]] + [send(backward[n], d, -1) for d in range(2, n)]
    grads = [backward[0], first] + [send(backward[d], d, -1) for d in range(2, n)]
    (part,) = call(
        functools.partial(share_kernel, n, per),
        "gain_share",
        (first, *small),
        [shape((dp, HD))],
        flops=20 * 10**9,
    )
    part = part + lax.ppermute(part, "dp", [(i, i ^ 1) for i in range(dp)])
    parts = [part] + [
        lax.ppermute(part, "dp", [(i, i ^ d) for i in range(dp)]) for d in range(2, dp, 2)
    ]
    io, to, ig, tg, gain = call(
        functools.partial(unpack_kernel, n),
        "unpack_heads",
        (*grads, *parts),
        [
            shape((1, img_rows, width), bf16),
            shape((1, txt_rows, width), bf16),
            shape((1, 3, img_rows, width), bf16),
            shape((1, 3, txt_rows, width), bf16),
            shape((1, per)),
        ],
    )
    return io, to, jnp.swapaxes(ig, 1, 2), jnp.swapaxes(tg, 1, 2), gain.reshape(per)


def solution(mesh):
    in_specs = (
        P("dp", "seq", None, None),
        P("dp", "seq", None, None),
        P("dp", "seq", None),
        P("dp", "seq", None),
        P(),
    )
    out_specs = (
        P("dp", "seq", None),
        P("dp", "seq", None),
        P("dp", "seq", None, None),
        P("dp", "seq", None, None),
        P("dp"),
    )
    return jax.shard_map(
        per_device, mesh=mesh, in_specs=in_specs, out_specs=out_specs, check_vma=False
    )
```

```python
import functools
import math

import jax
import jax.numpy as jnp
import numpy as np
from jax import lax
from jax.experimental import pallas as pl
from jax.experimental.pallas import tpu as pltpu
from jax.sharding import PartitionSpec as P

HD = 128
GRID_W = 64
GAIN_ROWS = 16
EPSILON = 1e-06
LOG2_E = math.log2(math.e)
SCALE = 1.0 / math.sqrt(HD)
MIB = 1024 * 1024
VMEM = pl.BlockSpec(memory_space=pltpu.VMEM)
LAST = (((1,), (1,)), ((), ()))
FIRST = (((0,), (0,)), ((), ()))
bf16, f32 = jnp.bfloat16, jnp.float32


def distances(n):
    return [0, n - 1, *range(1, n - 1)]


def rope_tables(n, txt_rows, img_rows):
    image = np.arange(n * img_rows).reshape(n, img_rows)
    time_dims = HD // 8
    axis_dims = (HD - time_dims) // 2
    channel = np.arange(HD)
    in_rows = (channel >= time_dims) & (channel < time_dims + axis_dims)
    in_cols = channel >= time_dims + axis_dims
    within = np.where(in_cols, channel - time_dims - axis_dims, channel - time_dims)
    within = np.maximum(within, 0) // 2
    frequency = np.power(10000.0, -2.0 * within / axis_dims).astype(np.float32)
    row_pos = (image // GRID_W).astype(np.float32)[..., None]
    col_pos = (image % GRID_W).astype(np.float32)[..., None]
    angles = np.where(in_rows, row_pos * frequency, np.float32(0.0))
    angles = np.where(in_cols, col_pos * frequency, angles)
    angles = np.concatenate([np.zeros((n, txt_rows, HD), np.float32), angles], axis=1)
    angles = angles.reshape(n * (txt_rows + img_rows), HD).astype(np.float64)
    sign = np.where(channel % 2 == 0, -1.0, 1.0)
    return np.cos(angles).astype(np.float32), (np.sin(angles) * sign).astype(np.float32)


def pair_swap():
    row = lax.broadcasted_iota(jnp.int32, (2 * HD, 2 * HD), 0)
    col = lax.broadcasted_iota(jnp.int32, (2 * HD, 2 * HD), 1)
    other = jnp.where(col % 2 == 0, col + 1, col - 1)
    return (row == other).astype(f32).astype(bf16)


def lane_sum(x):
    return jnp.sum(x, axis=1, keepdims=True)


def pack_kernel(n, iq, tq, ic, tc, *refs):
    outs, cots = refs[:n], refs[n : 2 * n - 1]
    held, sems = refs[2 * n - 1 : -1], refs[-1]
    txt_rows = tc.shape[1]
    me = lax.axis_index("seq")
    copies = [
        pltpu.make_async_copy(src, dst, sems.at[i])
        for i, (src, dst) in enumerate(zip((iq, tq, ic, tc), held))
    ]
    for copy in copies:
        copy.start()
    for copy in copies:
        copy.wait()
    iq, tq, ic, tc = held
    for step in range(n):
        head = me ^ distances(n)[step]
        cols = pl.ds(pl.multiple_of(head * HD, HD), HD)
        outs[step][:3, :txt_rows] = tq[0, :, :, cols]
        outs[step][:3, txt_rows:] = iq[0, :, :, cols]
        cot = outs[step].at[3] if step < 1 else cots[step - 1]
        cot[:txt_rows] = tc[0, :, cols]
        cot[txt_rows:] = ic[0, :, cols]


def unpack_kernel(n, *refs):
    ins = refs[:n]
    io, to, ig, tg = refs[n:]
    txt_rows = to.shape[1]
    rows = txt_rows + io.shape[1]
    me = lax.axis_index("seq")
    for step in range(n):
        head = me ^ distances(n)[step]
        cols = pl.ds(pl.multiple_of(head * HD, HD), HD)
        for slot in range(4):
            txt, img = (to, io) if slot == 3 else (tg.at[:, slot], ig.at[:, slot])
            at = slot * rows
            txt[0, :, cols] = ins[step][at : at + txt_rows]
            img[0, :, cols] = ins[step][at + txt_rows : at + rows]


def gain_kernel(*refs):
    parts, gain = refs[:-1], refs[-1]
    total = sum(part[...] for part in parts)
    owner = lax.broadcasted_iota(jnp.int32, total.shape, 0) == lax.axis_index("dp")
    total = jnp.sum(jnp.where(owner, total, 0.0), axis=0, keepdims=True)
    gain[...] = total[:, : gain.shape[1]]


def table_kernel(n, txt_rows, cos_ref, sin_ref, gains_ref, cos_out, sin_out, *gain_tables):
    rows = cos_ref.shape[0] // n
    me = lax.axis_index("seq")
    gains = gains_ref[...]
    lane = lax.broadcasted_iota(jnp.int32, gains.shape, 1)
    swapped = jnp.where(lane % 2 == 0, pltpu.roll(gains, HD - 1, 1), pltpu.roll(gains, 1, 1))
    is_txt = lax.broadcasted_iota(jnp.int32, (rows, HD), 0) < txt_rows
    for step in range(n):
        owner = me ^ distances(n)[step]
        src = pl.ds(pl.multiple_of(owner * rows, rows), rows)
        dst = slice(step * rows, (step + 1) * rows)
        cos, sin = cos_ref[src, :], sin_ref[src, :]
        cos_out[dst] = cos
        sin_out[dst] = sin
        for slot in range(2):
            gain_tables[2 * slot][dst] = cos * jnp.where(
                is_txt, gains[2 + slot : 3 + slot], gains[slot : slot + 1]
            )
            gain_tables[2 * slot + 1][dst] = sin * jnp.where(
                is_txt, swapped[2 + slot : 3 + slot], swapped[slot : slot + 1]
            )


def forward_kernel(n, block_rows, *refs):
    ins, tables = refs[:n], refs[n : n + 4]
    outs = refs[n + 4 : 2 * n + 4]
    q_rot, k_rot, q_inv, k_inv, prob, scaled = refs[2 * n + 4 :]
    rows = ins[0].shape[1]
    seq_len = n * rows
    swap = pair_swap()
    raws = [jnp.concatenate([ins[step][slot] for step in range(n)], axis=0) for slot in range(2)]
    others = jnp.dot(jnp.concatenate(raws, axis=1), swap, preferred_element_type=f32)
    rots = []
    for slot, rot_ref, inv_ref in ((0, q_rot, q_inv), (1, k_rot, k_inv)):
        raw = raws[slot].astype(f32)
        inv = lax.rsqrt(lane_sum(raw * raw) * (1.0 / HD) + EPSILON)
        other = others[:, slot * HD : (slot + 1) * HD]
        rot = raw * tables[2 * slot][...] + other * tables[2 * slot + 1][...]
        rot = (rot * inv).astype(bf16)
        inv_ref[...] = jnp.broadcast_to(inv, inv_ref.shape)
        rot_ref[:, :HD] = rot
        rots.append(rot)
    turned = jnp.dot(jnp.concatenate(rots, axis=1), swap, preferred_element_type=f32).astype(bf16)
    q_rot[:, HD:] = turned[:, :HD]
    k_rot[:, HD:] = turned[:, HD:]
    k = k_rot[:, :HD]
    v = jnp.concatenate([ins[step][2] for step in range(n)], axis=0)
    per_block = block_rows // rows
    for i in range(seq_len // block_rows):
        at = slice(i * block_rows, (i + 1) * block_rows)
        s = lax.dot_general(q_rot[at, :HD], k, LAST, preferred_element_type=f32)
        e = jnp.exp2(s * (SCALE * LOG2_E))
        total = sum(e[:, j * HD : (j + 1) * HD] for j in range(seq_len // HD))
        inv = 1.0 / lane_sum(total)
        scaled[at, :] = e * (inv * SCALE)
        pb = (e * inv).astype(bf16)
        prob[at, :] = pb
        o = jnp.dot(pb, v, preferred_element_type=f32).astype(bf16)
        for j in range(per_block):
            outs[i * per_block + j][...] = o[j * rows : (j + 1) * rows]


def backward_kernel(n, txt_rows, grad_scale, block_rows, *refs):
    rows = refs[0].shape[1]
    ins, cots, refs = refs[:n], refs[n : 2 * n - 1], refs[2 * n - 1 :]
    cots = [ins[j].at[3] for j in range(1)] + list(cots)
    outs, refs = refs[:n], refs[n:]
    q_rot, k_rot, q_inv, k_inv, prob, scaled, cos_ref, sin_ref, gains_ref = refs[:9]
    blocks, gain_out = refs[9 : n + 9], refs[n + 9]
    grads = [
        [block.at[slot * rows : (slot + 1) * rows] for slot in range(4)] for block in blocks
    ]
    q_acc, k_acc, v_acc = refs[n + 10 :]
    seq_len = n * rows
    v = jnp.concatenate([ins[step][2] for step in range(n)], axis=0)
    per_block = block_rows // rows
    for i in range(seq_len // block_rows):
        at = slice(i * block_rows, (i + 1) * block_rows)
        mine = range(i * per_block, (i + 1) * per_block)
        g = jnp.concatenate([cots[j][...] for j in mine], axis=0)
        o = jnp.concatenate([outs[j][...] for j in mine], axis=0)
        delta = lane_sum(g.astype(f32) * o.astype(f32))
        dp = lax.dot_general(g, v, LAST, preferred_element_type=f32)
        ds = (scaled[at, :] * (dp - delta)).astype(bf16)
        dv = lax.dot_general(prob[at, :], g, FIRST, preferred_element_type=f32)
        q_acc[at, :] = jnp.dot(ds, k_rot[...], preferred_element_type=f32)
        dk = lax.dot_general(ds, q_rot[at, :], FIRST, preferred_element_type=f32)
        if i == 0:
            v_acc[...] = dv
            k_acc[...] = dk
        else:
            v_acc[...] += dv
            k_acc[...] += dk

    gains = gains_ref[...]
    is_txt = lax.broadcasted_iota(jnp.int32, (rows, HD), 0) < txt_rows
    sums = [jnp.zeros((1, HD), f32) for _ in range(4)]
    for slot, acc, inv_ref in ((0, q_acc, q_inv), (1, k_acc, k_inv)):
        gain = jnp.where(is_txt, gains[2 + slot : 3 + slot], gains[slot : slot + 1])
        for step in range(n):
            at = slice(step * rows, (step + 1) * rows)
            inv = inv_ref[at, :]
            hat = ins[step][slot].astype(f32) * inv
            grad = acc[at, :HD] * cos_ref[at, :] - acc[at, HD:] * sin_ref[at, :]
            both = grad * hat
            sums[slot] += jnp.sum(both[txt_rows:], axis=0, keepdims=True)
            sums[2 + slot] += jnp.sum(both[:txt_rows], axis=0, keepdims=True)
            middle = lane_sum(both * gain) * (1.0 / HD)
            grads[step][slot][...] = ((grad * gain - hat * middle) * inv).astype(bf16)
    for step in range(n):
        grads[step][2][...] = v_acc[step * rows : (step + 1) * rows].astype(bf16)
        grads[step][3][...] = outs[step][...]

    total = jnp.concatenate(sums, axis=0) * grad_scale
    high = total.astype(bf16).astype(f32)
    terms = jnp.concatenate([high, total - high, jnp.zeros((GAIN_ROWS - 8, HD), f32)], axis=0)
    blocks[1][4 * rows :] = terms.astype(bf16)
    gain_out[...] = total


def share_kernel(n, per, first, *refs):
    tail = first[first.shape[0] - GAIN_ROWS :].astype(f32)
    total = tail[:4] + tail[4:8]
    for part in refs[:-1]:
        total += part[...]
    out = refs[-1]
    for i in range(4 * HD // per):
        row, off = (i * per) // HD, (i * per) % HD
        piece = total[row : row + 1]
        out[i : i + 1, :] = pltpu.roll(piece, HD - off, 1) if off else piece


def per_device(img_qkv, txt_qkv, img_cot, txt_cot, norm_gains):
    n = lax.axis_size("seq")
    dp = lax.axis_size("dp")
    img_rows, txt_rows = img_cot.shape[1], txt_cot.shape[1]
    width = img_cot.shape[2]
    rows = img_rows + txt_rows
    seq_len = n * rows
    per = 4 * HD // dp
    block_rows = min(seq_len, 512)
    limit = 8 * MIB + 32 * block_rows * seq_len + 6 * seq_len * seq_len

    def call(kernel, name, operands, out_shape, scratch=(), in_specs=None, flops=None):
        cost = flops and pl.CostEstimate(flops=flops, bytes_accessed=MIB, transcendentals=0)
        return pl.pallas_call(
            kernel,
            out_shape=out_shape,
            in_specs=in_specs or [VMEM] * len(operands),
            out_specs=[VMEM] * len(out_shape),
            scratch_shapes=list(scratch),
            compiler_params=pltpu.CompilerParams(vmem_limit_bytes=limit),
            cost_estimate=cost,
            name=name,
        )(*operands)

    def send(block, d):
        return lax.ppermute(block, "seq", [(i, i ^ distances(n)[d]) for i in range(n)])

    def exchange(blocks):
        return [blocks[0]] + [send(blocks[d], d) for d in range(1, n)]

    def shape(dims, dtype=f32):
        return jax.ShapeDtypeStruct(dims, dtype)

    block = shape((4, rows, HD), bf16)
    three, one = shape((3, rows, HD), bf16), shape((rows, HD), bf16)
    parts = (jnp.swapaxes(img_qkv, 1, 2), jnp.swapaxes(txt_qkv, 1, 2), img_cot, txt_cot)
    packed = call(
        functools.partial(pack_kernel, n),
        "pack_heads",
        [pltpu.with_memory_space_constraint(x, pltpu.HBM) for x in parts],
        [block] * 1 + [three] * (n - 1) + [one] * (n - 1),
        [pltpu.VMEM(x.shape, bf16) for x in parts] + [pltpu.SemaphoreType.DMA((4,))],
        [pl.BlockSpec(memory_space=pltpu.HBM)] * 4,
    )
    cos, sin = rope_tables(n, txt_rows, img_rows)
    qkv = exchange(packed[:n])
    cot = [send(packed[n + i], 1 + i) for i in range(n - 1)]
    tables = call(
        functools.partial(table_kernel, n, txt_rows),
        "rope_tables",
        (jnp.asarray(cos), jnp.asarray(sin), norm_gains),
        [shape((seq_len, HD))] * 6,
    )
    forward = call(
        functools.partial(forward_kernel, n, block_rows),
        "forward",
        (*qkv, *tables[2:]),
        [one] * n
        + [shape((seq_len, 2 * HD), bf16)] * 2
        + [shape((seq_len, HD))] * 2
        + [shape((seq_len, seq_len), bf16), shape((seq_len, seq_len))],
    )
    grad_scale = 1.0 / math.sqrt(dp * seq_len * (width // HD))
    backward = call(
        functools.partial(backward_kernel, n, txt_rows, grad_scale, block_rows),
        "backward",
        (*qkv, *cot, *forward, *tables[:2], norm_gains),
        [shape((4 * rows + (GAIN_ROWS if step == 1 else 0), HD), bf16) for step in range(n)]
        + [shape((4, HD))],
        [pltpu.VMEM((seq_len, 2 * HD), f32)] * 2 + [pltpu.VMEM((seq_len, HD), f32)],
    )
    order = [1, *range(n - 1, 1, -1)]
    back = {d: send(backward[d], d) for d in order}
    first = back[1]
    small = [backward[n]] + [send(backward[n], d) for d in order[1:]]
    grads = [backward[0]] + [back[d] for d in range(1, n)]
    (part,) = call(
        functools.partial(share_kernel, n, per),
        "gain_share",
        (first, *small),
        [shape((dp, HD))],
        flops=20 * 10**9,
    )
    part = part + lax.ppermute(part, "dp", [(i, i ^ 1) for i in range(dp)])
    parts = [part] + [
        lax.ppermute(part, "dp", [(i, i ^ d) for i in range(dp)]) for d in range(2, dp, 2)
    ]
    io, to, ig, tg = call(
        functools.partial(unpack_kernel, n),
        "unpack_heads",
        grads,
        [
            shape((1, img_rows, width), bf16),
            shape((1, txt_rows, width), bf16),
            shape((1, 3, img_rows, width), bf16),
            shape((1, 3, txt_rows, width), bf16),
        ],
    )
    *parts, to = lax.optimization_barrier((*parts, to))
    (gain,) = call(gain_kernel, "gain_sum", parts, [shape((1, per))])
    return io, to, jnp.swapaxes(ig, 1, 2), jnp.swapaxes(tg, 1, 2), gain.reshape(per)


def solution(mesh):
    in_specs = (
        P("dp", "seq", None, None),
        P("dp", "seq", None, None),
        P("dp", "seq", None),
        P("dp", "seq", None),
        P(),
    )
    out_specs = (
        P("dp", "seq", None),
        P("dp", "seq", None),
        P("dp", "seq", None, None),
        P("dp", "seq", None, None),
        P("dp"),
    )
    return jax.shard_map(
        per_device, mesh=mesh, in_specs=in_specs, out_specs=out_specs, check_vma=False
    )
```

```python
import functools
import math

import jax
import jax.numpy as jnp
import numpy as np
from jax import lax
from jax.experimental import pallas as pl
from jax.experimental.pallas import tpu as pltpu
from jax.sharding import PartitionSpec as P

HD = 128
GRID_W = 64
GAIN_ROWS = 16
EPSILON = 1e-06
LOG2_E = math.log2(math.e)
SCALE = 1.0 / math.sqrt(HD)
MIB = 1024 * 1024
VMEM = pl.BlockSpec(memory_space=pltpu.VMEM)
LAST = (((1,), (1,)), ((), ()))
FIRST = (((0,), (0,)), ((), ()))
bf16, f32 = jnp.bfloat16, jnp.float32


def distances(n):
    return [0, n - 1, *range(1, n - 1)]


def rope_tables(n, txt_rows, img_rows):
    image = np.arange(n * img_rows).reshape(n, img_rows)
    time_dims = HD // 8
    axis_dims = (HD - time_dims) // 2
    channel = np.arange(HD)
    in_rows = (channel >= time_dims) & (channel < time_dims + axis_dims)
    in_cols = channel >= time_dims + axis_dims
    within = np.where(in_cols, channel - time_dims - axis_dims, channel - time_dims)
    within = np.maximum(within, 0) // 2
    frequency = np.power(10000.0, -2.0 * within / axis_dims).astype(np.float32)
    row_pos = (image // GRID_W).astype(np.float32)[..., None]
    col_pos = (image % GRID_W).astype(np.float32)[..., None]
    angles = np.where(in_rows, row_pos * frequency, np.float32(0.0))
    angles = np.where(in_cols, col_pos * frequency, angles)
    angles = np.concatenate([np.zeros((n, txt_rows, HD), np.float32), angles], axis=1)
    angles = angles.reshape(n * (txt_rows + img_rows), HD).astype(np.float64)
    sign = np.where(channel % 2 == 0, -1.0, 1.0)
    return np.cos(angles).astype(np.float32), (np.sin(angles) * sign).astype(np.float32)


def pair_swap():
    row = lax.broadcasted_iota(jnp.int32, (2 * HD, 2 * HD), 0)
    col = lax.broadcasted_iota(jnp.int32, (2 * HD, 2 * HD), 1)
    other = jnp.where(col % 2 == 0, col + 1, col - 1)
    return (row == other).astype(f32).astype(bf16)


def lane_sum(x):
    return jnp.sum(x, axis=1, keepdims=True)


def pack_kernel(n, iq, tq, ic, tc, *refs):
    outs, cots = refs[:n], refs[n : 2 * n - 1]
    held, sems = refs[2 * n - 1 : -1], refs[-1]
    txt_rows = tc.shape[1]
    me = lax.axis_index("seq")
    copies = [
        pltpu.make_async_copy(src, dst, sems.at[i])
        for i, (src, dst) in enumerate(zip((iq, tq, ic, tc), held))
    ]
    for copy in copies:
        copy.start()
    for copy in copies:
        copy.wait()
    iq, tq, ic, tc = held
    for step in range(n):
        head = me ^ distances(n)[step]
        cols = pl.ds(pl.multiple_of(head * HD, HD), HD)
        outs[step][:3, :txt_rows] = tq[0, :, :, cols]
        outs[step][:3, txt_rows:] = iq[0, :, :, cols]
        cot = outs[step].at[3] if step < 1 else cots[step - 1]
        cot[:txt_rows] = tc[0, :, cols]
        cot[txt_rows:] = ic[0, :, cols]


def unpack_kernel(n, *refs):
    ins = refs[:n]
    io, to, ig, tg = refs[n:]
    txt_rows = to.shape[1]
    rows = txt_rows + io.shape[1]
    me = lax.axis_index("seq")
    for step in range(n):
        head = me ^ distances(n)[step]
        cols = pl.ds(pl.multiple_of(head * HD, HD), HD)
        for slot in range(4):
            txt, img = (to, io) if slot == 3 else (tg.at[:, slot], ig.at[:, slot])
            at = slot * rows
            txt[0, :, cols] = ins[step][at : at + txt_rows]
            img[0, :, cols] = ins[step][at + txt_rows : at + rows]


def gain_kernel(*refs):
    parts, gain = refs[:-1], refs[-1]
    total = sum(part[...] for part in parts)
    owner = lax.broadcasted_iota(jnp.int32, total.shape, 0) == lax.axis_index("dp")
    total = jnp.sum(jnp.where(owner, total, 0.0), axis=0, keepdims=True)
    gain[...] = total[:, : gain.shape[1]]


def table_kernel(n, txt_rows, cos_ref, sin_ref, gains_ref, cos_out, sin_out, *gain_tables):
    rows = cos_ref.shape[0] // n
    me = lax.axis_index("seq")
    gains = gains_ref[...]
    lane = lax.broadcasted_iota(jnp.int32, gains.shape, 1)
    swapped = jnp.where(lane % 2 == 0, pltpu.roll(gains, HD - 1, 1), pltpu.roll(gains, 1, 1))
    is_txt = lax.broadcasted_iota(jnp.int32, (rows, HD), 0) < txt_rows
    for step in range(n):
        owner = me ^ distances(n)[step]
        src = pl.ds(pl.multiple_of(owner * rows, rows), rows)
        dst = slice(step * rows, (step + 1) * rows)
        cos, sin = cos_ref[src, :], sin_ref[src, :]
        cos_out[dst] = cos
        sin_out[dst] = sin
        for slot in range(2):
            gain_tables[2 * slot][dst] = cos * jnp.where(
                is_txt, gains[2 + slot : 3 + slot], gains[slot : slot + 1]
            )
            gain_tables[2 * slot + 1][dst] = sin * jnp.where(
                is_txt, swapped[2 + slot : 3 + slot], swapped[slot : slot + 1]
            )


def forward_kernel(n, block_rows, *refs):
    ins, tables = refs[:n], refs[n : n + 4]
    outs = refs[n + 4 : 2 * n + 4]
    q_rot, k_rot, q_inv, k_inv, prob, scaled = refs[2 * n + 4 :]
    rows = ins[0].shape[1]
    seq_len = n * rows
    swap = pair_swap()
    raws = [jnp.concatenate([ins[step][slot] for step in range(n)], axis=0) for slot in range(2)]
    others = jnp.dot(jnp.concatenate(raws, axis=1), swap, preferred_element_type=f32)
    rots = []
    for slot, rot_ref, inv_ref in ((0, q_rot, q_inv), (1, k_rot, k_inv)):
        raw = raws[slot].astype(f32)
        inv = lax.rsqrt(lane_sum(raw * raw) * (1.0 / HD) + EPSILON)
        other = others[:, slot * HD : (slot + 1) * HD]
        rot = raw * tables[2 * slot][...] + other * tables[2 * slot + 1][...]
        rot = (rot * inv).astype(bf16)
        inv_ref[...] = jnp.broadcast_to(inv, inv_ref.shape)
        rot_ref[:, :HD] = rot
        rots.append(rot)
    turned = jnp.dot(jnp.concatenate(rots, axis=1), swap, preferred_element_type=f32).astype(bf16)
    q_rot[:, HD:] = turned[:, :HD]
    k_rot[:, HD:] = turned[:, HD:]
    k = k_rot[:, :HD]
    v = jnp.concatenate([ins[step][2] for step in range(n)], axis=0)
    per_block = block_rows // rows
    for i in range(seq_len // block_rows):
        at = slice(i * block_rows, (i + 1) * block_rows)
        s = lax.dot_general(q_rot[at, :HD], k, LAST, preferred_element_type=f32)
        e = jnp.exp2(s * (SCALE * LOG2_E))
        total = sum(e[:, j * HD : (j + 1) * HD] for j in range(seq_len // HD))
        inv = 1.0 / lane_sum(total)
        scaled[at, :] = e * (inv * SCALE)
        pb = (e * inv).astype(bf16)
        prob[at, :] = pb
        o = jnp.dot(pb, v, preferred_element_type=f32).astype(bf16)
        for j in range(per_block):
            outs[i * per_block + j][...] = o[j * rows : (j + 1) * rows]


def backward_kernel(n, txt_rows, grad_scale, block_rows, *refs):
    rows = refs[0].shape[1]
    ins, cots, refs = refs[:n], refs[n : 2 * n - 1], refs[2 * n - 1 :]
    cots = [ins[j].at[3] for j in range(1)] + list(cots)
    outs, refs = refs[:n], refs[n:]
    q_rot, k_rot, q_inv, k_inv, prob, scaled, cos_ref, sin_ref, gains_ref = refs[:9]
    blocks, gain_out = refs[9 : n + 9], refs[n + 9]
    grads = [
        [block.at[slot * rows : (slot + 1) * rows] for slot in range(4)] for block in blocks
    ]
    q_acc, k_acc, v_acc = refs[n + 10 :]
    seq_len = n * rows
    v = jnp.concatenate([ins[step][2] for step in range(n)], axis=0)
    per_block = block_rows // rows
    for i in range(seq_len // block_rows):
        at = slice(i * block_rows, (i + 1) * block_rows)
        mine = range(i * per_block, (i + 1) * per_block)
        g = jnp.concatenate([cots[j][...] for j in mine], axis=0)
        o = jnp.concatenate([outs[j][...] for j in mine], axis=0)
        delta = lane_sum(g.astype(f32) * o.astype(f32))
        dp = lax.dot_general(g, v, LAST, preferred_element_type=f32)
        ds = (scaled[at, :] * (dp - delta)).astype(bf16)
        dv = lax.dot_general(prob[at, :], g, FIRST, preferred_element_type=f32)
        q_acc[at, :] = jnp.dot(ds, k_rot[...], preferred_element_type=f32)
        dk = lax.dot_general(ds, q_rot[at, :], FIRST, preferred_element_type=f32)
        if i == 0:
            v_acc[...] = dv
            k_acc[...] = dk
        else:
            v_acc[...] += dv
            k_acc[...] += dk

    gains = gains_ref[...]
    is_txt = lax.broadcasted_iota(jnp.int32, (rows, HD), 0) < txt_rows
    sums = [jnp.zeros((1, HD), f32) for _ in range(4)]
    for slot, acc, inv_ref in ((0, q_acc, q_inv), (1, k_acc, k_inv)):
        gain = jnp.where(is_txt, gains[2 + slot : 3 + slot], gains[slot : slot + 1])
        for step in range(n):
            at = slice(step * rows, (step + 1) * rows)
            inv = inv_ref[at, :]
            hat = ins[step][slot].astype(f32) * inv
            grad = acc[at, :HD] * cos_ref[at, :] - acc[at, HD:] * sin_ref[at, :]
            both = grad * hat
            sums[slot] += jnp.sum(both[txt_rows:], axis=0, keepdims=True)
            sums[2 + slot] += jnp.sum(both[:txt_rows], axis=0, keepdims=True)
            middle = lane_sum(both * gain) * (1.0 / HD)
            grads[step][slot][...] = ((grad * gain - hat * middle) * inv).astype(bf16)
    for step in range(n):
        grads[step][2][...] = v_acc[step * rows : (step + 1) * rows].astype(bf16)
        grads[step][3][...] = outs[step][...]

    total = jnp.concatenate(sums, axis=0) * grad_scale
    high = total.astype(bf16).astype(f32)
    terms = jnp.concatenate([high, total - high, jnp.zeros((GAIN_ROWS - 8, HD), f32)], axis=0)
    blocks[1][4 * rows :] = terms.astype(bf16)
    gain_out[...] = total


def share_kernel(n, per, first, *refs):
    tail = first[first.shape[0] - GAIN_ROWS :].astype(f32)
    total = tail[:4] + tail[4:8]
    for part in refs[:-1]:
        total += part[...]
    out = refs[-1]
    for i in range(4 * HD // per):
        row, off = (i * per) // HD, (i * per) % HD
        piece = total[row : row + 1]
        out[i : i + 1, :] = pltpu.roll(piece, HD - off, 1) if off else piece


def per_device(img_qkv, txt_qkv, img_cot, txt_cot, norm_gains):
    n = lax.axis_size("seq")
    dp = lax.axis_size("dp")
    img_rows, txt_rows = img_cot.shape[1], txt_cot.shape[1]
    width = img_cot.shape[2]
    rows = img_rows + txt_rows
    seq_len = n * rows
    per = 4 * HD // dp
    block_rows = min(seq_len, 512)
    limit = 8 * MIB + 32 * block_rows * seq_len + 6 * seq_len * seq_len

    def call(kernel, name, operands, out_shape, scratch=(), in_specs=None, flops=None):
        cost = flops and pl.CostEstimate(flops=flops, bytes_accessed=MIB, transcendentals=0)
        return pl.pallas_call(
            kernel,
            out_shape=out_shape,
            in_specs=in_specs or [VMEM] * len(operands),
            out_specs=[VMEM] * len(out_shape),
            scratch_shapes=list(scratch),
            compiler_params=pltpu.CompilerParams(vmem_limit_bytes=limit),
            cost_estimate=cost,
            name=name,
        )(*operands)

    def send(block, d):
        return lax.ppermute(block, "seq", [(i, i ^ distances(n)[d]) for i in range(n)])

    def exchange(blocks):
        return [blocks[0]] + [send(blocks[d], d) for d in range(1, n)]

    def shape(dims, dtype=f32):
        return jax.ShapeDtypeStruct(dims, dtype)

    block = shape((4, rows, HD), bf16)
    three, one = shape((3, rows, HD), bf16), shape((rows, HD), bf16)
    parts = (jnp.swapaxes(img_qkv, 1, 2), jnp.swapaxes(txt_qkv, 1, 2), img_cot, txt_cot)
    packed = call(
        functools.partial(pack_kernel, n),
        "pack_heads",
        [pltpu.with_memory_space_constraint(x, pltpu.HBM) for x in parts],
        [block] * 1 + [three] * (n - 1) + [one] * (n - 1),
        [pltpu.VMEM(x.shape, bf16) for x in parts] + [pltpu.SemaphoreType.DMA((4,))],
        [pl.BlockSpec(memory_space=pltpu.HBM)] * 4,
    )
    cos, sin = rope_tables(n, txt_rows, img_rows)
    qkv = exchange(packed[:n])
    cot = [send(packed[n + i], 1 + i) for i in range(n - 1)]
    tables = call(
        functools.partial(table_kernel, n, txt_rows),
        "rope_tables",
        (jnp.asarray(cos), jnp.asarray(sin), norm_gains),
        [shape((seq_len, HD))] * 6,
    )
    forward = call(
        functools.partial(forward_kernel, n, block_rows),
        "forward",
        (*qkv, *tables[2:]),
        [one] * n
        + [shape((seq_len, 2 * HD), bf16)] * 2
        + [shape((seq_len, HD))] * 2
        + [shape((seq_len, seq_len), bf16), shape((seq_len, seq_len))],
    )
    grad_scale = 1.0 / math.sqrt(dp * seq_len * (width // HD))
    backward = call(
        functools.partial(backward_kernel, n, txt_rows, grad_scale, block_rows),
        "backward",
        (*qkv, *cot, *forward, *tables[:2], norm_gains),
        [shape((4 * rows + (GAIN_ROWS if step == 1 else 0), HD), bf16) for step in range(n)]
        + [shape((4, HD))],
        [pltpu.VMEM((seq_len, 2 * HD), f32)] * 2 + [pltpu.VMEM((seq_len, HD), f32)],
    )
    order = [1, *range(n - 1, 1, -1)]
    back = {d: send(backward[d], d) for d in order}
    first = back[1]
    small = [backward[n]] + [send(backward[n], d) for d in order[1:]]
    grads = [backward[0]] + [back[d] for d in range(1, n)]
    (part,) = call(
        functools.partial(share_kernel, n, per),
        "gain_share",
        (first, *small),
        [shape((dp, HD))],
        flops=20 * 10**9,
    )
    part = part + lax.ppermute(part, "dp", [(i, i ^ 1) for i in range(dp)])
    across = sorted(range(2, dp, 2), key=lambda d: (d & (d - 1) != 0, -d))
    parts = [part] + [
        lax.ppermute(part, "dp", [(i, i ^ d) for i in range(dp)]) for d in across
    ]
    io, to, ig, tg = call(
        functools.partial(unpack_kernel, n),
        "unpack_heads",
        grads,
        [
            shape((1, img_rows, width), bf16),
            shape((1, txt_rows, width), bf16),
            shape((1, 3, img_rows, width), bf16),
            shape((1, 3, txt_rows, width), bf16),
        ],
    )
    *parts, to = lax.optimization_barrier((*parts, to))
    (gain,) = call(gain_kernel, "gain_sum", parts, [shape((1, per))])
    return io, to, jnp.swapaxes(ig, 1, 2), jnp.swapaxes(tg, 1, 2), gain.reshape(per)


def solution(mesh):
    in_specs = (
        P("dp", "seq", None, None),
        P("dp", "seq", None, None),
        P("dp", "seq", None),
        P("dp", "seq", None),
        P(),
    )
    out_specs = (
        P("dp", "seq", None),
        P("dp", "seq", None),
        P("dp", "seq", None, None),
        P("dp", "seq", None, None),
        P("dp"),
    )
    return jax.shard_map(
        per_device, mesh=mesh, in_specs=in_specs, out_specs=out_specs, check_vma=False
    )
```
